1024 devices in a mesh: tile: 128 (over y, z), depth: 8 (over x, core).
Axes of the slice: x: 4, y: 8, z: 16, core: 2. Of those that a mesh axis runs over, the one named last changes fastest.
Arguments:
- volume: bfloat16 [2048, 256, 2048], P('tile', 'depth'), may hold values from -4 to 4
Outputs:
- image: float32 [4, 2048, 2048], P(None, ('tile', 'depth'))
The draws below stay inside these ranges and needn't reach their ends.
All inputs are finite; a program needn't handle non-finite values.
Results may differ from the reference program's by a relative error of at most 0.0003.
Values may be sent and summed in bfloat16 or wider, within the bound.
A program may use at most 32 MiB of HBM per device.

```python
import jax
import jax.numpy as jnp
from jax import lax

CX = 16
CZ = 32
NY = 2048
NX = 2048
NZ = 256
N_TILE = 128
N_DEPTH = 8


def steps_of(key, shape, split, smallest, top_value):
    level = 1.0
    for position, blocks in split:
        steps = jax.random.uniform(jax.random.fold_in(jax.random.fold_in(key, 6), position), (blocks,), jnp.float32, smallest / len(split), top_value / len(split))
        level = level * jnp.repeat(jnp.exp(steps), shape[position] // blocks).reshape((-1,) + (1,) * (len(shape) - 1 - position))
    return level


def noise(rng, shape, width, limit, split=(), kind=jnp.bfloat16):
    drawn = jax.random.normal(rng, shape, jnp.float32) * width
    if len(split) > 0:
        drawn = steps_of(rng, shape, split, -0.22, 0.18) * drawn
    return jnp.clip(drawn, min=-limit, max=limit).astype(kind)


def setup_inputs(seed: int = 0) -> dict:
    keys = jax.random.split(jax.random.key(seed), 2)
    volume = noise(keys[0], (NX, NZ, NY), 1.0, 4.0, ((0, 128), (1, 8)))
    return dict(volume=volume)


OPACITY = 3.0
LIGHT_X = 0.48
LIGHT_Y = 0.6
LIGHT_Z = 0.64

def brick_image(padded, depth_total):
    field = padded.astype(jnp.float32)
    center = field[1:-1, 1:-1, 1:-1]
    grad_x = 0.5 * (field[2:, 1:-1, 1:-1] - field[:-2, 1:-1, 1:-1])
    grad_z = 0.5 * (field[1:-1, 2:, 1:-1] - field[1:-1, :-2, 1:-1])
    grad_y = 0.5 * (field[1:-1, 1:-1, 2:] - field[1:-1, 1:-1, :-2])
    facing = LIGHT_X * grad_x + LIGHT_Y * grad_y + LIGHT_Z * grad_z
    shade = 0.3 + 0.7 * jnp.abs(facing) / jnp.sqrt(1.0 + grad_x * grad_x + grad_y * grad_y + grad_z * grad_z)
    squared = center * center
    extinct = OPACITY / depth_total * squared / (1.0 + squared)
    before = jnp.cumsum(extinct, axis=1) - extinct
    weight = jnp.exp(-before) * (1.0 - jnp.exp(-extinct)) * shade
    red = lax.optimization_barrier(jnp.sum(weight * jax.nn.sigmoid(2.0 * center), axis=1))
    green = lax.optimization_barrier(jnp.sum(weight * (0.5 * jnp.exp(-squared)), axis=1))
    blue = lax.optimization_barrier(jnp.sum(weight * jax.nn.sigmoid(-2.0 * center), axis=1))
    passing = jnp.exp(-lax.optimization_barrier(jnp.sum(extinct, axis=1)))
    return jnp.stack([red, green, blue, passing], 0)

def reference(volume):
    padded = jnp.pad(volume, 1)

    def strip(column):
        slab = lax.dynamic_slice_in_dim(padded, (column * CX).astype(jnp.int32), CX + 2, 0)
        colour = jnp.zeros((3, CX, NY), jnp.float32)
        passing = jnp.ones((1, CX, NY), jnp.float32)
        for brick in range(N_DEPTH):
            part = brick_image(slab[:, brick * CZ:brick * CZ + CZ + 2, :], NZ)
            colour = colour + passing * part[:3]
            passing = passing * part[3:]
        return jnp.concatenate([colour, 1.0 - passing], 0)
    strips = lax.map(strip, jnp.arange(N_TILE, dtype=jnp.int32))
    return jnp.transpose(strips, (1, 0, 2, 3)).reshape(4, NX, NY)
```

```python
import functools
import math

import jax
import jax.numpy as jnp
from jax import lax
from jax.experimental import pallas as pl
from jax.experimental.pallas import tpu as pltpu
from jax.sharding import PartitionSpec as P

OPACITY = 3.0
LIGHT_X = 0.48
LIGHT_Y = 0.6
LIGHT_Z = 0.64
LOG2E = math.log2(math.e)
SHADE = 0.7 * LIGHT_Z
UNROLL = 4


def column_terms(rate, centre, x_pair, y_diff, z_pair, state):
    run, light, total, skew, green = state
    gx = x_pair[1] - x_pair[0]
    gz = z_pair[1] - z_pair[0]
    gy = y_diff
    facing = jnp.abs(gz + (LIGHT_X / LIGHT_Z) * gx + (LIGHT_Y / LIGHT_Z) * gy)
    norm = lax.rsqrt((gx * gx + 4.0) + (gy * gy + gz * gz))
    shade = facing * norm + 0.3 / SHADE
    squared = centre * centre
    run = run + squared * pl_reciprocal(1.0 + squared)
    after = jnp.exp2(run * (-rate))
    weight = (light - after) * shade
    total = total + weight
    skew = skew + weight * jnp.tanh(centre)
    green = green + weight * jnp.exp2(squared * (-LOG2E))
    return run, after, total, skew, green


def pl_reciprocal(value):
    return pltpu.reciprocal(value, approx=True)


def y_differences(first, second, lane, row):
    above = jnp.where(row == 7, 0.0, pltpu.roll(first, 7, 0))
    below = jnp.where(row == 0, 0.0, pltpu.roll(second, 1, 0))
    right_0 = pltpu.roll(jnp.where(lane == 0, second, first), 127, 1)
    right_1 = pltpu.roll(jnp.where(lane == 0, above, second), 127, 1)
    left_0 = pltpu.roll(jnp.where(lane == 127, below, first), 1, 1)
    left_1 = pltpu.roll(jnp.where(lane == 127, first, second), 1, 1)
    return right_0 - left_0, right_1 - left_1


def relayout(order, slab):
    stacked = jnp.concatenate([slab[:, 256 * c : 256 * c + 256] for c in range(8)], axis=0)
    return jnp.dot(order, stacked, preferred_element_type=jnp.float32)


def render_kernel(
    tiles, depths, v_ref, o_ref, vin, ws, zout, zin, part, recv,
    load_sem, xs_sem, xr_sem, zs_sem, zr_sem, ps_sem, pr_sem,
):
    MESH = pl.DeviceIdType.MESH
    cx, cz, _ = v_ref.shape
    tile = lax.axis_index("tile")
    me = lax.axis_index("depth")
    tile_up, tile_down = lax.rem(tile + 1, tiles), lax.rem(tile + tiles - 1, tiles)
    deep_up, deep_down = lax.rem(me + 1, depths), lax.rem(me + depths - 1, depths)
    rate = OPACITY / (cz * depths) * LOG2E

    barrier = pltpu.get_barrier_semaphore()
    for other in (tile_up, tile_down):
        pl.semaphore_signal(barrier, inc=1, device_id={"tile": other}, device_id_type=MESH)
    for step in range(1, depths):
        pl.semaphore_signal(
            barrier, inc=1, device_id={"depth": lax.rem(me + step, depths)}, device_id_type=MESH
        )
    loads = []
    for i in range(4):
        n = cx // 4
        loads.append(
            pltpu.make_async_copy(
                v_ref.at[pl.ds(i * n, n)], vin.at[pl.ds(1 + i * n, n)], load_sem.at[i]
            )
        )
        loads[-1].start()
    in_row = lax.broadcasted_iota(jnp.int32, (256, 256), 1)
    out_row = lax.broadcasted_iota(jnp.int32, (256, 256), 0)
    wanted = (out_row % 8) * 32 + out_row // 8
    order = jnp.where(in_row == wanted, 1.0, 0.0).astype(jnp.bfloat16)

    pl.semaphore_wait(barrier, depths + 1)
    x_down = pltpu.make_async_remote_copy(
        v_ref.at[0], vin.at[cx + 1], xs_sem.at[0], xr_sem.at[0],
        device_id={"tile": tile_down}, device_id_type=MESH,
    )
    x_up = pltpu.make_async_remote_copy(
        v_ref.at[cx - 1], vin.at[0], xs_sem.at[1], xr_sem.at[1],
        device_id={"tile": tile_up}, device_id_type=MESH,
    )
    x_down.start()
    x_up.start()

    def own_slab(x, _):
        ws[x, pl.ds(8, 256), :] = relayout(order, vin[x])
        return 0

    for i in range(4):
        loads[i].wait()
        lax.fori_loop(1 + i * (cx // 4), 1 + (i + 1) * (cx // 4), own_slab, 0)

    def pack(x, _):
        for side, z in ((0, 1), (1, cz)):
            rows = ws[x + 1, pl.ds(8 * z, 8), :]
            zout[side, x] = jnp.concatenate([rows[:, :128], rows[:, 128:]], axis=0).astype(jnp.bfloat16)
        return 0

    lax.fori_loop(0, cx, pack, 0)
    z_down = pltpu.make_async_remote_copy(
        zout.at[0], zin.at[1], zs_sem.at[0], zr_sem.at[0],
        device_id={"depth": deep_down}, device_id_type=MESH,
    )
    z_up = pltpu.make_async_remote_copy(
        zout.at[1], zin.at[0], zs_sem.at[1], zr_sem.at[1],
        device_id={"depth": deep_up}, device_id_type=MESH,
    )
    z_down.start()
    z_up.start()

    x_down.wait_recv()
    x_up.wait_recv()
    keep_high = jnp.where(tile == tiles - 1, 0.0, 1.0)
    keep_low = jnp.where(tile == 0, 0.0, 1.0)
    ws[0, pl.ds(8, 256), :] = relayout(order, vin[0]) * keep_low
    ws[cx + 1, pl.ds(8, 256), :] = relayout(order, vin[cx + 1]) * keep_high
    z_down.wait_recv()
    z_up.wait_recv()
    near = jnp.where(me == 0, 0.0, 1.0)
    far = jnp.where(me == depths - 1, 0.0, 1.0)

    def unpack(x, _):
        for side, z, keep in ((0, 0, near), (1, cz + 1, far)):
            rows = zin[side, x].astype(jnp.float32) * keep
            ws[x + 1, pl.ds(8 * z, 8), :] = jnp.concatenate([rows[:8], rows[8:]], axis=1)
        return 0

    lax.fori_loop(0, cx, unpack, 0)

    lane = lax.broadcasted_iota(jnp.int32, (8, 128), 1)
    row = lax.broadcasted_iota(jnp.int32, (8, 128), 0)

    def group(d):
        first = 2 * d

        def cell(slab, z, h):
            start = 8 * z if isinstance(z, int) else pl.multiple_of(8 * z, 8)
            return ws[first + slab, pl.ds(start, 8), 128 * h : 128 * h + 128]

        def body(i, state):
            state = list(state)
            for u in range(UNROLL):
                z = i * UNROLL + u + 1
                for x in range(2):
                    centre = [cell(x + 1, z, h) for h in range(2)]
                    gy = y_differences(centre[0], centre[1], lane, row)
                    for h in range(2):
                        at = 2 * x + h
                        state[at] = column_terms(
                            rate,
                            centre[h],
                            (cell(x, z, h), cell(x + 2, z, h)),
                            gy[h],
                            (cell(x + 1, z - 1, h), cell(x + 1, z + 1, h)),
                            state[at],
                        )
            return tuple(state)

        zero = jnp.zeros((8, 128), jnp.float32)
        one = jnp.ones((8, 128), jnp.float32)
        state = tuple((zero, one, zero, zero, zero) for _ in range(4))
        state = lax.fori_loop(0, cz // UNROLL, body, state)
        for x in range(2):
            for h in range(2):
                run, _, total, skew, green = state[2 * x + h]
                for channel, value in enumerate((total, skew, green, run)):
                    part[d, channel, x, :, 128 * h : 128 * h + 128] = value

    def send(d):
        return pltpu.make_async_remote_copy(
            part.at[d], recv.at[me], ps_sem.at[d], pr_sem.at[me],
            device_id={"depth": d}, device_id_type=MESH,
        )

    def step(s, _):
        d = lax.rem(me + 1 + s, depths)
        group(d)

        @pl.when(s < depths - 1)
        def _():
            send(d).start()

        return 0

    lax.fori_loop(0, depths, step, 0)
    recv[me] = part[me]

    for s in range(1, depths):
        source = lax.rem(me + s, depths)
        pltpu.make_async_remote_copy(
            part.at[source], recv.at[source], ps_sem.at[source], pr_sem.at[source],
            device_id={"depth": source}, device_id_type=MESH,
        ).wait_recv()

    for x in range(2):
        run = recv[0, 3, x]
        total, skew, green = recv[0, 0, x], recv[0, 1, x], recv[0, 2, x]
        for k in range(1, depths):
            light = jnp.exp2(run * (-rate))
            total = total + light * recv[k, 0, x]
            skew = skew + light * recv[k, 1, x]
            green = green + light * recv[k, 2, x]
            run = run + recv[k, 3, x]
        half = 0.5 * SHADE
        o_ref[0, x] = half * (total + skew)
        o_ref[1, x] = half * green
        o_ref[2, x] = half * (total - skew)
        o_ref[3, x] = 1.0 - jnp.exp2(run * (-rate))

    x_down.wait_send()
    x_up.wait_send()
    z_down.wait_send()
    z_up.wait_send()
    for s in range(1, depths):
        send(lax.rem(me + s, depths)).wait_send()


def shards(volume):
    tiles, depths = lax.axis_size("tile"), lax.axis_size("depth")
    cx, cz, ny = volume.shape
    dma = pltpu.SemaphoreType.DMA
    image = pl.pallas_call(
        functools.partial(render_kernel, tiles, depths),
        out_shape=jax.ShapeDtypeStruct((4, cx // depths, 8, ny // 8), jnp.float32),
        in_specs=[pl.BlockSpec(memory_space=pltpu.HBM)],
        out_specs=pl.BlockSpec(memory_space=pltpu.VMEM),
        scratch_shapes=[
            pltpu.VMEM((cx + 2, cz, ny), jnp.bfloat16),
            pltpu.VMEM((cx + 2, 8 * (cz + 2), 256), jnp.float32),
            pltpu.VMEM((2, cx, 16, 128), jnp.bfloat16),
            pltpu.VMEM((2, cx, 16, 128), jnp.bfloat16),
            pltpu.VMEM((depths, 4, 2, 8, 256), jnp.float32),
            pltpu.VMEM((depths, 4, 2, 8, 256), jnp.float32),
            dma((4,)), dma((2,)), dma((2,)), dma((2,)), dma((2,)), dma((depths,)), dma((depths,)),
        ],
        compiler_params=pltpu.CompilerParams(
            collective_id=0, has_side_effects=True, vmem_limit_bytes=61 * 1024 * 1024
        ),
        cost_estimate=pl.CostEstimate(flops=50_000_000, bytes_accessed=2_300_000, transcendentals=5_000_000),
    )(volume)
    return image.reshape(4, cx // depths, ny)


def solution(mesh):
    in_specs = (P("tile", "depth", None),)
    out_specs = P(None, ("tile", "depth"), None)
    return jax.shard_map(shards, mesh=mesh, in_specs=in_specs, out_specs=out_specs, check_vma=False)
```

```python
import functools
import math

import jax
import jax.numpy as jnp
from jax import lax
from jax.experimental import pallas as pl
from jax.experimental.pallas import tpu as pltpu
from jax.sharding import PartitionSpec as P

OPACITY = 3.0
LIGHT_X = 0.48
LIGHT_Y = 0.6
LIGHT_Z = 0.64
LOG2E = math.log2(math.e)
SHADE = 0.7 * LIGHT_Z
PITCH = 16
LEAD = 8
EARLY = 3
MESH = pl.DeviceIdType.MESH


def plan(depths):
    early = min(EARLY, depths - 2)
    use = {}
    orders = []
    for me in range(depths):
        left = [(me + s) % depths for s in range(1, depths)]
        order = []
        for step in range(depths - 1):
            allowed = [d for d in left if step >= early or d not in (0, depths - 1)] or left
            pick = min(allowed, key=lambda d: (use.get((step, d), 0), (d - me) % depths))
            use[step, pick] = use.get((step, pick), 0) + 1
            order.append(pick)
            left.remove(pick)
        orders.append(order + [me])
    return orders


def choose(index, values):
    out = jnp.int32(values[0])
    for i in range(1, len(values)):
        out = jnp.where(index == i, jnp.int32(values[i]), out)
    return out


def cell_terms(rate, centre, gx, gy, gz, state):
    run, light, total, skew, green = state
    facing = jnp.abs(gz + (LIGHT_X / LIGHT_Z) * gx + (LIGHT_Y / LIGHT_Z) * gy)
    norm = lax.rsqrt((gx * gx + 4.0) + (gy * gy + gz * gz))
    shade = facing * norm + 0.3 / SHADE
    squared = centre * centre
    run = run + squared * pltpu.reciprocal(1.0 + squared, approx=True)
    after = jnp.exp2(run * (-rate))
    weight = (light - after) * shade
    total = total + weight
    skew = skew + weight * jnp.tanh(centre)
    green = green + weight * jnp.exp2(squared * (-LOG2E))
    return run, after, total, skew, green


def render_kernel(
    tiles, depths, v_ref, o_ref, vin, ws, zout, zin, part, recv,
    load_sem, xs_sem, xr_sem, zs_sem, zr_sem, ps_sem, pr_sem,
):
    cx, cz, _ = v_ref.shape
    tile = lax.axis_index("tile")
    me = lax.axis_index("depth")
    tile_up, tile_down = lax.rem(tile + 1, tiles), lax.rem(tile + tiles - 1, tiles)
    deep_up, deep_down = lax.rem(me + 1, depths), lax.rem(me + depths - 1, depths)
    rate = OPACITY / (cz * depths) * LOG2E

    barrier = pltpu.get_barrier_semaphore()
    for other in (tile_up, tile_down):
        pl.semaphore_signal(barrier, inc=1, device_id={"tile": other}, device_id_type=MESH)
    for step in range(1, depths):
        pl.semaphore_signal(
            barrier, inc=1, device_id={"depth": lax.rem(me + step, depths)}, device_id_type=MESH
        )
    loads = []
    batch = cx // 4
    for i in range(4):
        loads.append(
            pltpu.make_async_copy(
                v_ref.at[pl.ds(i * batch, batch)], vin.at[pl.ds(1 + i * batch, batch)], load_sem.at[i]
            )
        )
        loads[-1].start()
    in_row = lax.broadcasted_iota(jnp.int32, (256, 256), 1)
    out_row = lax.broadcasted_iota(jnp.int32, (256, 256), 0)
    order = jnp.where(in_row == (out_row % 8) * 32 + out_row // 8, 1.0, 0.0).astype(jnp.bfloat16)
    lane = lax.broadcasted_iota(jnp.int32, (8, 128), 1)
    zeros = jnp.zeros((8, 128), jnp.float32)

    def clear(x, _):
        for h in range(2):
            for z in range(cz + 1):
                ws[x, h, pl.ds(LEAD + PITCH * z - 8, 8), :] = zeros
        return 0

    lax.fori_loop(0, cx + 2, clear, 0)

    pl.semaphore_wait(barrier, depths + 1)
    x_down = pltpu.make_async_remote_copy(
        v_ref.at[0], vin.at[cx + 1], xs_sem.at[0], xr_sem.at[0],
        device_id={"tile": tile_down}, device_id_type=MESH,
    )
    x_up = pltpu.make_async_remote_copy(
        v_ref.at[cx - 1], vin.at[0], xs_sem.at[1], xr_sem.at[1],
        device_id={"tile": tile_up}, device_id_type=MESH,
    )
    x_down.start()
    x_up.start()

    def relayout(x, keep=None):
        slab = vin[x]
        stacked = jnp.concatenate([slab[:, 256 * c : 256 * c + 256] for c in range(8)], axis=0)
        out = jnp.dot(order, stacked, preferred_element_type=jnp.float32)
        if keep is not None:
            out = out * keep
        for z in range(cz):
            for h in range(2):
                ws[x, h, pl.ds(LEAD + PITCH * z, 8), :] = out[8 * z : 8 * z + 8, 128 * h : 128 * h + 128]

    def own_slabs(i, _):
        relayout(1 + 2 * i)
        relayout(2 + 2 * i)
        return 0

    for i in range(4):
        loads[i].wait()
        lax.fori_loop(i * (batch // 2), (i + 1) * (batch // 2), own_slabs, 0)

    def cell(slab, z, h, shift=0):
        return ws[slab, h, pl.ds(LEAD + PITCH * z + shift, 8), :]

    def pack(x, _):
        for side, z in ((0, 0), (1, cz - 1)):
            rows = jnp.concatenate([cell(x + 1, z, 0), cell(x + 1, z, 1)], axis=0)
            zout[side, x] = rows.astype(jnp.bfloat16)
        return 0

    lax.fori_loop(0, cx, pack, 0)
    z_down = pltpu.make_async_remote_copy(
        zout.at[0], zin.at[1], zs_sem.at[0], zr_sem.at[0],
        device_id={"depth": deep_down}, device_id_type=MESH,
    )
    z_up = pltpu.make_async_remote_copy(
        zout.at[1], zin.at[0], zs_sem.at[1], zr_sem.at[1],
        device_id={"depth": deep_up}, device_id_type=MESH,
    )
    z_down.start()
    z_up.start()

    def y_differences(slab, z):
        first, second = cell(slab, z, 0), cell(slab, z, 1)
        above, below = cell(slab, z, 0, 1), cell(slab, z, 1, -1)
        right_0 = pltpu.roll(jnp.where(lane == 0, second, first), 127, 1)
        right_1 = pltpu.roll(jnp.where(lane == 0, above, second), 127, 1)
        left_0 = pltpu.roll(jnp.where(lane == 127, below, first), 1, 1)
        left_1 = pltpu.roll(jnp.where(lane == 127, first, second), 1, 1)
        return right_0 - left_0, right_1 - left_1

    def inner(d):
        def column(x, _):
            slab = 2 * d + x + 1
            state = []
            for h in range(2):
                squared = cell(slab, 0, h) ** 2
                run = squared * pltpu.reciprocal(1.0 + squared, approx=True)
                state.append((run, jnp.exp2(run * (-rate)), zeros, zeros, zeros))
            for z in range(1, cz - 1):
                gy = y_differences(slab, z)
                for h in range(2):
                    state[h] = cell_terms(
                        rate,
                        cell(slab, z, h),
                        cell(slab + 1, z, h) - cell(slab - 1, z, h),
                        gy[h],
                        cell(slab, z + 1, h) - cell(slab, z - 1, h),
                        state[h],
                    )
            for h in range(2):
                run, _, total, skew, green = state[h]
                for channel, value in enumerate((total, skew, green, run)):
                    part[d, channel, x, h] = value
            return 0

        lax.fori_loop(0, 2, column, 0)

    near = jnp.where(me == 0, 0.0, 1.0)
    far = jnp.where(me == depths - 1, 0.0, 1.0)

    def outer(d):
        for x in range(2):
            slab = 2 * d + x + 1
            front = zin[0, slab - 1].astype(jnp.float32) * near
            back = zin[1, slab - 1].astype(jnp.float32) * far
            gy_first, gy_last = y_differences(slab, 0), y_differences(slab, cz - 1)
            for h in range(2):
                total, skew, green, run = (part[d, channel, x, h] for channel in range(4))
                _, _, total, skew, green = cell_terms(
                    rate,
                    cell(slab, 0, h),
                    cell(slab + 1, 0, h) - cell(slab - 1, 0, h),
                    gy_first[h],
                    cell(slab, 1, h) - front[8 * h : 8 * h + 8],
                    (zeros, 1.0, total, skew, green),
                )
                run, _, total, skew, green = cell_terms(
                    rate,
                    cell(slab, cz - 1, h),
                    cell(slab + 1, cz - 1, h) - cell(slab - 1, cz - 1, h),
                    gy_last[h],
                    back[8 * h : 8 * h + 8] - cell(slab, cz - 2, h),
                    (run, jnp.exp2(run * (-rate)), total, skew, green),
                )
                for channel, value in enumerate((total, skew, green, run)):
                    part[d, channel, x, h] = value

    def send(d):
        return pltpu.make_async_remote_copy(
            part.at[d], recv.at[me], ps_sem.at[d], pr_sem.at[me],
            device_id={"depth": d}, device_id_type=MESH,
        )

    codes = []
    orders = plan(depths)
    for s in range(depths):
        codes.append(sum(orders[k][s] * depths**k for k in range(depths)))
    power = choose(me, [depths**k for k in range(depths)])

    def target(s):
        return lax.rem(choose(s, codes) // power, depths)

    def finish(s, _):
        d = target(s)
        outer(d)

        @pl.when(s < depths - 1)
        def _():
            send(d).start()

        return 0

    def step(s, _):
        inner(target(s))

        @pl.when(s == 1)
        def _():
            z_down.wait_recv()
            z_up.wait_recv()

        @pl.when(s == EARLY - 1)
        def _():
            x_down.wait_recv()
            x_up.wait_recv()
            relayout(0, jnp.where(tile == 0, 0.0, 1.0))
            relayout(cx + 1, jnp.where(tile == tiles - 1, 0.0, 1.0))

        @pl.when(s >= 1)
        def _():
            lax.fori_loop(jnp.where(s == 1, 0, s), s + 1, finish, 0)

        return 0

    lax.fori_loop(0, depths, step, 0)
    recv[me] = part[me]

    for s in range(1, depths):
        source = lax.rem(me + s, depths)
        pltpu.make_async_remote_copy(
            part.at[source], recv.at[source], ps_sem.at[source], pr_sem.at[source],
            device_id={"depth": source}, device_id_type=MESH,
        ).wait_recv()

    half = 0.5 * SHADE
    for h in range(2):
        done = []
        for x in range(2):
            total, skew, green, run = (recv[0, channel, x, h] for channel in range(4))
            for k in range(1, depths):
                light = jnp.exp2(run * (-rate))
                total = total + light * recv[k, 0, x, h]
                skew = skew + light * recv[k, 1, x, h]
                green = green + light * recv[k, 2, x, h]
                run = run + recv[k, 3, x, h]
            done.append(
                (half * (total + skew), half * green, half * (total - skew), 1.0 - jnp.exp2(run * (-rate)))
            )
        for channel in range(4):
            for c in range(8):
                rows = [done[x][channel][c : c + 1] for x in range(2)]
                o_ref[channel, :, 256 * c + 128 * h : 256 * c + 128 * h + 128] = jnp.concatenate(rows, axis=0)

    x_down.wait_send()
    x_up.wait_send()
    z_down.wait_send()
    z_up.wait_send()
    for s in range(1, depths):
        send(lax.rem(me + s, depths)).wait_send()


def shards(volume):
    tiles, depths = lax.axis_size("tile"), lax.axis_size("depth")
    cx, cz, ny = volume.shape
    dma = pltpu.SemaphoreType.DMA
    return pl.pallas_call(
        functools.partial(render_kernel, tiles, depths),
        out_shape=jax.ShapeDtypeStruct((4, cx // depths, ny), jnp.float32),
        in_specs=[pl.BlockSpec(memory_space=pltpu.HBM)],
        out_specs=pl.BlockSpec(memory_space=pltpu.VMEM),
        scratch_shapes=[
            pltpu.VMEM((cx + 2, cz, ny), jnp.bfloat16),
            pltpu.VMEM((cx + 2, 2, LEAD + PITCH * cz, 128), jnp.float32),
            pltpu.VMEM((2, cx, 16, 128), jnp.bfloat16),
            pltpu.VMEM((2, cx, 16, 128), jnp.bfloat16),
            pltpu.VMEM((depths, 4, 2, 2, 8, 128), jnp.float32),
            pltpu.VMEM((depths, 4, 2, 2, 8, 128), jnp.float32),
            dma((4,)), dma((2,)), dma((2,)), dma((2,)), dma((2,)), dma((depths,)), dma((depths,)),
        ],
        compiler_params=pltpu.CompilerParams(
            collective_id=0, has_side_effects=True, vmem_limit_bytes=61 * 1024 * 1024
        ),
        cost_estimate=pl.CostEstimate(flops=50_000_000, bytes_accessed=2_300_000, transcendentals=5_000_000),
    )(volume)


def solution(mesh):
    in_specs = (P("tile", "depth", None),)
    out_specs = P(None, ("tile", "depth"), None)
    return jax.shard_map(shards, mesh=mesh, in_specs=in_specs, out_specs=out_specs, check_vma=False)
```

```python
import functools
import math

import jax
import jax.numpy as jnp
from jax import lax
from jax.experimental import pallas as pl
from jax.experimental.pallas import tpu as pltpu
from jax.sharding import PartitionSpec as P

OPACITY = 3.0
LIGHT_X = 0.48
LIGHT_Y = 0.6
LIGHT_Z = 0.64
LOG2E = math.log2(math.e)
SHADE = 0.7 * LIGHT_Z
PITCH = 16
LEAD = 8
EARLY = 4
FIRST = 3
POWER = 12
SCALES = (256.0, 512.0, 256.0, 32.0)
MESH = pl.DeviceIdType.MESH


def plan(depths):
    use = {}
    orders = []
    chips = depths // 2
    for me in range(depths):

        def hops(d):
            apart = abs(d // 2 - me // 2)
            return min(apart, chips - apart)

        left = [d for d in range(depths) if d != me]
        order = []
        for step in range(depths - 1):
            allowed = [d for d in left if hops(d) > 0 or len(left) == 1]
            allowed = [d for d in allowed if step >= EARLY or d not in (0, depths - 1)] or left
            pick = min(allowed, key=lambda d: (use.get((step, d), 0) - hops(d), (d - me) % depths))
            use[step, pick] = use.get((step, pick), 0) + 1
            order.append(pick)
            left.remove(pick)
        orders.append(order + [me])
    return orders


def choose(index, values):
    out = jnp.int32(values[0])
    for i in range(1, len(values)):
        out = jnp.where(index == i, jnp.int32(values[i]), out)
    return out


def encode(value, scale):
    value = value * scale
    fourth = (value * value) * (value * value)
    return fourth * fourth * fourth


def decode(code, scale):
    return jnp.exp2(jnp.log2(code.astype(jnp.float32)) * (1.0 / POWER) - math.log2(scale))


def cell_terms(rate, centre, gx, gy, gz, state):
    run, light, total, skew, green = state
    facing = jnp.abs(gz + (LIGHT_X / LIGHT_Z) * gx + (LIGHT_Y / LIGHT_Z) * gy)
    norm = lax.rsqrt((gx * gx + 4.0) + (gy * gy + gz * gz))
    shade = facing * norm + 0.3 / SHADE
    squared = centre * centre
    run = run + squared * pltpu.reciprocal(1.0 + squared, approx=True)
    after = jnp.exp2(run * (-rate))
    weight = (light - after) * shade
    total = total + weight
    skew = skew + weight * jnp.tanh(centre)
    green = green + weight * jnp.exp2(squared * (-LOG2E))
    return run, after, total, skew, green


def render_kernel(
    tiles, depths, v_ref, o_ref, vin, ws, zout, zin, part, coded, recv,
    load_sem, xs_sem, xr_sem, zs_sem, zr_sem, ps_sem, pr_sem,
):
    cx, cz, _ = v_ref.shape
    tile = lax.axis_index("tile")
    me = lax.axis_index("depth")
    tile_up, tile_down = lax.rem(tile + 1, tiles), lax.rem(tile + tiles - 1, tiles)
    deep_up, deep_down = lax.rem(me + 1, depths), lax.rem(me + depths - 1, depths)
    rate = OPACITY / (cz * depths) * LOG2E

    barrier = pltpu.get_barrier_semaphore()
    for other in (tile_up, tile_down):
        pl.semaphore_signal(barrier, inc=1, device_id={"tile": other}, device_id_type=MESH)
    for step in range(1, depths):
        pl.semaphore_signal(
            barrier, inc=1, device_id={"depth": lax.rem(me + step, depths)}, device_id_type=MESH
        )
    loads = []
    batch = cx // 4
    for i in range(4):
        loads.append(
            pltpu.make_async_copy(
                v_ref.at[pl.ds(i * batch, batch)], vin.at[pl.ds(1 + i * batch, batch)], load_sem.at[i]
            )
        )
        loads[-1].start()
    in_row = lax.broadcasted_iota(jnp.int32, (256, 256), 1)
    out_row = lax.broadcasted_iota(jnp.int32, (256, 256), 0)
    order = jnp.where(in_row == (out_row % 8) * 32 + out_row // 8, 1.0, 0.0).astype(jnp.bfloat16)
    lane = lax.broadcasted_iota(jnp.int32, (8, 128), 1)
    zeros = jnp.zeros((8, 128), jnp.float32)

    def clear(x, _):
        for h in range(2):
            for z in range(cz + 1):
                ws[x, h, pl.ds(LEAD + PITCH * z - 8, 8), :] = zeros
        return 0

    lax.fori_loop(0, cx + 2, clear, 0)

    x_down = pltpu.make_async_remote_copy(
        v_ref.at[0], vin.at[cx + 1], xs_sem.at[0], xr_sem.at[0],
        device_id={"tile": tile_down}, device_id_type=MESH,
    )
    x_up = pltpu.make_async_remote_copy(
        v_ref.at[cx - 1], vin.at[0], xs_sem.at[1], xr_sem.at[1],
        device_id={"tile": tile_up}, device_id_type=MESH,
    )
    def relayout(x, keep=None):
        slab = vin[x]
        stacked = jnp.concatenate([slab[:, 256 * c : 256 * c + 256] for c in range(8)], axis=0)
        out = jnp.dot(order, stacked, preferred_element_type=jnp.float32)
        if keep is not None:
            out = out * keep
        for z in range(cz):
            for h in range(2):
                ws[x, h, pl.ds(LEAD + PITCH * z, 8), :] = out[8 * z : 8 * z + 8, 128 * h : 128 * h + 128]

    def own_slabs(i):
        for x in range(batch):
            relayout(1 + batch * i + x)

    for i in range(4):
        loads[i].wait()
        own_slabs(i)
        if i == 1:
            pl.semaphore_wait(barrier, depths + 1)
            x_down.start()
            x_up.start()

    def cell(slab, z, h, shift=0):
        return ws[slab, h, pl.ds(LEAD + PITCH * z + shift, 8), :]

    def pack(x, _):
        for side, z in ((0, 0), (1, cz - 1)):
            rows = jnp.concatenate([cell(x + 1, z, 0), cell(x + 1, z, 1)], axis=0)
            zout[side, x] = rows.astype(jnp.bfloat16)
        return 0

    lax.fori_loop(0, cx, pack, 0)
    z_down = pltpu.make_async_remote_copy(
        zout.at[0], zin.at[1], zs_sem.at[0], zr_sem.at[0],
        device_id={"depth": deep_down}, device_id_type=MESH,
    )
    z_up = pltpu.make_async_remote_copy(
        zout.at[1], zin.at[0], zs_sem.at[1], zr_sem.at[1],
        device_id={"depth": deep_up}, device_id_type=MESH,
    )
    z_down.start()
    z_up.start()

    def y_differences(slab, z):
        first, second = cell(slab, z, 0), cell(slab, z, 1)
        above, below = cell(slab, z, 0, 1), cell(slab, z, 1, -1)
        right_0 = pltpu.roll(jnp.where(lane == 0, second, first), 127, 1)
        right_1 = pltpu.roll(jnp.where(lane == 0, above, second), 127, 1)
        left_0 = pltpu.roll(jnp.where(lane == 127, below, first), 1, 1)
        left_1 = pltpu.roll(jnp.where(lane == 127, first, second), 1, 1)
        return right_0 - left_0, right_1 - left_1

    def inner(d):
        def column(x, _):
            slab = 2 * d + x + 1
            state = []
            for h in range(2):
                squared = cell(slab, 0, h) ** 2
                run = squared * pltpu.reciprocal(1.0 + squared, approx=True)
                state.append((run, jnp.exp2(run * (-rate)), zeros, zeros, zeros))
            for z in range(1, cz - 1):
                gy = y_differences(slab, z)
                for h in range(2):
                    state[h] = cell_terms(
                        rate,
                        cell(slab, z, h),
                        cell(slab + 1, z, h) - cell(slab - 1, z, h),
                        gy[h],
                        cell(slab, z + 1, h) - cell(slab, z - 1, h),
                        state[h],
                    )
            for h in range(2):
                run, _, total, skew, green = state[h]
                for channel, value in enumerate((total, skew, green, run)):
                    part[d, channel, x, h] = value
            return 0

        lax.fori_loop(0, 2, column, 0)

    near = jnp.where(me == 0, 0.0, 1.0)
    far = jnp.where(me == depths - 1, 0.0, 1.0)

    def outer(d):
        for x in range(2):
            slab = 2 * d + x + 1
            front = zin[0, slab - 1].astype(jnp.float32) * near
            back = zin[1, slab - 1].astype(jnp.float32) * far
            gy_first, gy_last = y_differences(slab, 0), y_differences(slab, cz - 1)
            for h in range(2):
                total, skew, green, run = (part[d, channel, x, h] for channel in range(4))
                _, _, total, skew, green = cell_terms(
                    rate,
                    cell(slab, 0, h),
                    cell(slab + 1, 0, h) - cell(slab - 1, 0, h),
                    gy_first[h],
                    cell(slab, 1, h) - front[8 * h : 8 * h + 8],
                    (zeros, 1.0, total, skew, green),
                )
                run, _, total, skew, green = cell_terms(
                    rate,
                    cell(slab, cz - 1, h),
                    cell(slab + 1, cz - 1, h) - cell(slab - 1, cz - 1, h),
                    gy_last[h],
                    back[8 * h : 8 * h + 8] - cell(slab, cz - 2, h),
                    (run, jnp.exp2(run * (-rate)), total, skew, green),
                )
                for channel, value in enumerate((total + skew, green, total - skew, run)):
                    part[d, channel, x, h] = value
            for channel in range(4):
                rows = [encode(part[d, channel, x, h], SCALES[channel]) for h in range(2)]
                coded[d, channel, x] = jnp.concatenate(rows, axis=0).astype(jnp.bfloat16)

    def send(d):
        return pltpu.make_async_remote_copy(
            coded.at[d], recv.at[me], ps_sem.at[d], pr_sem.at[me],
            device_id={"depth": d}, device_id_type=MESH,
        )

    codes = []
    orders = plan(depths)
    for s in range(depths):
        codes.append(sum(orders[k][s] * depths**k for k in range(depths)))
    power = choose(me, [depths**k for k in range(depths)])

    def target(s):
        return lax.rem(choose(s, codes) // power, depths)

    def finish(s, _):
        d = target(s)
        outer(d)

        @pl.when(s < depths - 1)
        def _():
            send(d).start()

        return 0

    def step(s, _):
        inner(target(s))

        @pl.when(s == FIRST - 1)
        def _():
            z_down.wait_recv()
            z_up.wait_recv()

        @pl.when(s == EARLY - 1)
        def _():
            x_down.wait_recv()
            x_up.wait_recv()
            relayout(0, jnp.where(tile == 0, 0.0, 1.0))
            relayout(cx + 1, jnp.where(tile == tiles - 1, 0.0, 1.0))

        @pl.when(s >= FIRST - 1)
        def _():
            lax.fori_loop(jnp.where(s == FIRST - 1, 0, s), s + 1, finish, 0)

        return 0

    lax.fori_loop(0, depths, step, 0)
    recv[me] = coded[me]

    for s in range(1, depths):
        source = lax.rem(me + s, depths)
        pltpu.make_async_remote_copy(
            coded.at[source], recv.at[source], ps_sem.at[source], pr_sem.at[source],
            device_id={"depth": source}, device_id_type=MESH,
        ).wait_recv()

    for x in range(2):
        run = jnp.zeros((16, 128), jnp.float32)
        colours = [run, run, run]
        for k in range(depths):
            light = jnp.exp2(run * (-rate))
            for channel in range(3):
                colours[channel] += light * decode(recv[k, channel, x], SCALES[channel])
            run = run + decode(recv[k, 3, x], SCALES[3])
        image = [0.5 * SHADE * colour for colour in colours] + [1.0 - jnp.exp2(run * (-rate))]
        for channel in range(4):
            for h in range(2):
                for c in range(8):
                    y = 256 * c + 128 * h
                    o_ref[channel, x : x + 1, y : y + 128] = image[channel][8 * h + c : 8 * h + c + 1]

    x_down.wait_send()
    x_up.wait_send()
    z_down.wait_send()
    z_up.wait_send()
    for s in range(1, depths):
        send(lax.rem(me + s, depths)).wait_send()


def shards(volume):
    tiles, depths = lax.axis_size("tile"), lax.axis_size("depth")
    cx, cz, ny = volume.shape
    dma = pltpu.SemaphoreType.DMA
    return pl.pallas_call(
        functools.partial(render_kernel, tiles, depths),
        out_shape=jax.ShapeDtypeStruct((4, cx // depths, ny), jnp.float32),
        in_specs=[pl.BlockSpec(memory_space=pltpu.HBM)],
        out_specs=pl.BlockSpec(memory_space=pltpu.VMEM),
        scratch_shapes=[
            pltpu.VMEM((cx + 2, cz, ny), jnp.bfloat16),
            pltpu.VMEM((cx + 2, 2, LEAD + PITCH * cz, 128), jnp.float32),
            pltpu.VMEM((2, cx, 16, 128), jnp.bfloat16),
            pltpu.VMEM((2, cx, 16, 128), jnp.bfloat16),
            pltpu.VMEM((depths, 4, 2, 2, 8, 128), jnp.float32),
            pltpu.VMEM((depths, 4, 2, 16, 128), jnp.bfloat16),
            pltpu.VMEM((depths, 4, 2, 16, 128), jnp.bfloat16),
            dma((4,)), dma((2,)), dma((2,)), dma((2,)), dma((2,)), dma((depths,)), dma((depths,)),
        ],
        compiler_params=pltpu.CompilerParams(
            collective_id=0, has_side_effects=True, vmem_limit_bytes=52 * 1024 * 1024
        ),
        cost_estimate=pl.CostEstimate(flops=50_000_000, bytes_accessed=2_300_000, transcendentals=5_000_000),
    )(volume)


def solution(mesh):
    in_specs = (P("tile", "depth", None),)
    out_specs = P(None, ("tile", "depth"), None)
    return jax.shard_map(shards, mesh=mesh, in_specs=in_specs, out_specs=out_specs, check_vma=False)
```

```python
import functools
import math

import jax
import jax.numpy as jnp
from jax import lax
from jax.experimental import pallas as pl
from jax.experimental.pallas import tpu as pltpu
from jax.sharding import PartitionSpec as P

OPACITY = 3.0
LIGHT_X = 0.48
LIGHT_Y = 0.6
LIGHT_Z = 0.64
LOG2E = math.log2(math.e)
SHADE = 0.7 * LIGHT_Z
PITCH = 16
LEAD = 8
EARLY = 5
FIRST = 3
POWER = 12
SCALES = (256.0, 512.0, 256.0, 32.0)
MESH = pl.DeviceIdType.MESH


def plan(depths):
    use = {}
    orders = []
    chips = depths // 2
    for me in range(depths):

        def hops(d):
            apart = abs(d // 2 - me // 2)
            return min(apart, chips - apart)

        left = [d for d in range(depths) if d != me]
        order = []
        for step in range(depths - 1):
            allowed = [d for d in left if step >= EARLY or d not in (0, depths - 1)]
            allowed = [d for d in allowed if hops(d) > 0] or allowed
            pick = min(allowed, key=lambda d: (use.get((step, d), 0) - hops(d), (d - me) % depths))
            use[step, pick] = use.get((step, pick), 0) + 1
            order.append(pick)
            left.remove(pick)
        orders.append(order + [me])
    return orders


def choose(index, values):
    out = jnp.int32(values[0])
    for i in range(1, len(values)):
        out = jnp.where(index == i, jnp.int32(values[i]), out)
    return out


def encode(value, scale):
    value = value * scale
    fourth = (value * value) * (value * value)
    return fourth * fourth * fourth


def decode(code, scale):
    return jnp.exp2(jnp.log2(code.astype(jnp.float32)) * (1.0 / POWER) - math.log2(scale))


def cell_terms(rate, centre, gx, gy, gz, state):
    run, light, total, skew, green = state
    facing = jnp.abs((gz + (LIGHT_X / LIGHT_Z) * gx) + (LIGHT_Y / LIGHT_Z) * gy)
    norm = lax.rsqrt(((gx * gx + 4.0) + gz * gz) + gy * gy)
    shade = facing * norm + 0.3 / SHADE
    squared = centre * centre
    run = run + squared * pltpu.reciprocal(1.0 + squared, approx=True)
    after = jnp.exp2(run * (-rate))
    weight = (light - after) * shade
    total = total + weight
    skew = skew + weight * jnp.tanh(centre)
    green = green + weight * jnp.exp2(squared * (-LOG2E))
    return run, after, total, skew, green


def render_kernel(
    tiles, depths, v_ref, o_ref, vin, ws, zout, zin, part, coded, recv,
    load_sem, xs_sem, xr_sem, zs_sem, zr_sem, ps_sem, pr_sem,
):
    cx, cz, _ = v_ref.shape
    tile = lax.axis_index("tile")
    me = lax.axis_index("depth")
    tile_up, tile_down = lax.rem(tile + 1, tiles), lax.rem(tile + tiles - 1, tiles)
    has_up, has_down = tile < tiles - 1, tile > 0
    deep_up, deep_down = lax.rem(me + 1, depths), lax.rem(me + depths - 1, depths)
    rate = OPACITY / (cz * depths) * LOG2E

    barrier = pltpu.get_barrier_semaphore()
    for other, there in ((tile_up, has_up), (tile_down, has_down)):

        @pl.when(there)
        def _():
            pl.semaphore_signal(barrier, inc=1, device_id={"tile": other}, device_id_type=MESH)

    for step in range(1, depths):
        pl.semaphore_signal(
            barrier, inc=1, device_id={"depth": lax.rem(me + step, depths)}, device_id_type=MESH
        )
    loads = []
    batch = cx // 4
    for i in range(4):
        loads.append(
            pltpu.make_async_copy(
                v_ref.at[pl.ds(i * batch, batch)], vin.at[pl.ds(1 + i * batch, batch)], load_sem.at[i]
            )
        )
        loads[-1].start()
    in_row = lax.broadcasted_iota(jnp.int32, (256, 256), 1)
    out_row = lax.broadcasted_iota(jnp.int32, (256, 256), 0)
    order = jnp.where(in_row == (out_row % 8) * 32 + out_row // 8, 1.0, 0.0).astype(jnp.bfloat16)
    lane = lax.broadcasted_iota(jnp.int32, (8, 128), 1)
    zeros = jnp.zeros((8, 128), jnp.float32)

    def clear(x, _):
        for h in range(2):
            for z in range(cz + 1):
                ws[x, h, pl.ds(LEAD + PITCH * z - 8, 8), :] = zeros
        return 0

    lax.fori_loop(0, cx + 2, clear, 0)
    for x, there in ((0, has_down), (cx + 1, has_up)):

        @pl.when(jnp.logical_not(there))
        def _():
            for h in range(2):
                for z in range(cz):
                    ws[x, h, pl.ds(LEAD + PITCH * z, 8), :] = zeros


    x_down = pltpu.make_async_remote_copy(
        v_ref.at[0], vin.at[cx + 1], xs_sem.at[0], xr_sem.at[0],
        device_id={"tile": tile_down}, device_id_type=MESH,
    )
    x_up = pltpu.make_async_remote_copy(
        v_ref.at[cx - 1], vin.at[0], xs_sem.at[1], xr_sem.at[1],
        device_id={"tile": tile_up}, device_id_type=MESH,
    )
    def relayout(x):
        slab = vin[x]
        stacked = jnp.concatenate([slab[:, 256 * c : 256 * c + 256] for c in range(8)], axis=0)
        out = jnp.dot(order, stacked, preferred_element_type=jnp.float32)
        for z in range(cz):
            for h in range(2):
                ws[x, h, pl.ds(LEAD + PITCH * z, 8), :] = out[8 * z : 8 * z + 8, 128 * h : 128 * h + 128]

    def own_slabs(i):
        for x in range(batch):
            relayout(1 + batch * i + x)

    for i in range(4):
        loads[i].wait()
        own_slabs(i)
        if i == 1:
            pl.semaphore_wait(barrier, depths - 1 + jnp.where(has_up, 1, 0) + jnp.where(has_down, 1, 0))
            pl.when(has_down)(x_down.start)
            pl.when(has_up)(x_up.start)

    def cell(slab, z, h, shift=0):
        return ws[slab, h, pl.ds(LEAD + PITCH * z + shift, 8), :]

    def pack(x, _):
        for side, z in ((0, 0), (1, cz - 1)):
            rows = jnp.concatenate([cell(x + 1, z, 0), cell(x + 1, z, 1)], axis=0)
            zout[side, x] = rows.astype(jnp.bfloat16)
        return 0

    lax.fori_loop(0, cx, pack, 0)
    z_down = pltpu.make_async_remote_copy(
        zout.at[0], zin.at[1], zs_sem.at[0], zr_sem.at[0],
        device_id={"depth": deep_down}, device_id_type=MESH,
    )
    z_up = pltpu.make_async_remote_copy(
        zout.at[1], zin.at[0], zs_sem.at[1], zr_sem.at[1],
        device_id={"depth": deep_up}, device_id_type=MESH,
    )
    z_down.start()
    z_up.start()

    def y_differences(slab, z):
        first, second = cell(slab, z, 0), cell(slab, z, 1)
        above, below = cell(slab, z, 0, 1), cell(slab, z, 1, -1)
        right_0 = pltpu.roll(jnp.where(lane == 0, second, first), 127, 1)
        right_1 = pltpu.roll(jnp.where(lane == 0, above, second), 127, 1)
        left_0 = pltpu.roll(jnp.where(lane == 127, below, first), 1, 1)
        left_1 = pltpu.roll(jnp.where(lane == 127, first, second), 1, 1)
        return right_0 - left_0, right_1 - left_1

    near = jnp.where(me == 0, 0.0, 1.0)
    far = jnp.where(me == depths - 1, 0.0, 1.0)

    def x_difference(slab, z, h):
        return cell(slab + 1, z, h) - cell(slab - 1, z, h)

    def front_layer(slab, state):
        halo = zin[0, slab - 1].astype(jnp.float32) * near
        gy = y_differences(slab, 0)
        out = []
        for h in range(2):
            gz = cell(slab, 1, h) - halo[8 * h : 8 * h + 8]
            out.append(cell_terms(rate, cell(slab, 0, h), x_difference(slab, 0, h), gy[h], gz, state[h]))
        return out

    def back_layer(slab, state):
        halo = zin[1, slab - 1].astype(jnp.float32) * far
        gy = y_differences(slab, cz - 1)
        out = []
        for h in range(2):
            gz = halo[8 * h : 8 * h + 8] - cell(slab, cz - 2, h)
            out.append(
                cell_terms(rate, cell(slab, cz - 1, h), x_difference(slab, cz - 1, h), gy[h], gz, state[h])
            )
        return out

    def inner_layers(slab, state):
        for z in range(1, cz - 1):
            gy = y_differences(slab, z)
            for h in range(2):
                gz = cell(slab, z + 1, h) - cell(slab, z - 1, h)
                state[h] = cell_terms(rate, cell(slab, z, h), x_difference(slab, z, h), gy[h], gz, state[h])
        return state

    def store(d, x, state):
        pairs = []
        for run, _, total, skew, green in state:
            pairs.append([encode(v, s) for v, s in zip((total + skew, green, total - skew, run), SCALES)])
        for channel in range(4):
            rows = jnp.concatenate([pairs[0][channel], pairs[1][channel]], axis=0)
            coded[d, channel, x] = rows.astype(jnp.bfloat16)

    def inner(d):
        def column(x, _):
            slab = 2 * d + x + 1
            state = []
            for h in range(2):
                squared = cell(slab, 0, h) ** 2
                run = squared * pltpu.reciprocal(1.0 + squared, approx=True)
                state.append((run, jnp.exp2(run * (-rate)), zeros, zeros, zeros))
            state = inner_layers(slab, state)
            for h in range(2):
                run, _, total, skew, green = state[h]
                for channel, value in enumerate((total, skew, green, run)):
                    part[d, channel, x, h] = value
            return 0

        lax.fori_loop(0, 2, column, 0)

    def outer(d):
        for x in range(2):
            slab = 2 * d + x + 1
            state = []
            for h in range(2):
                total, skew, green, run = (part[d, channel, x, h] for channel in range(4))
                state.append((zeros, 1.0, total, skew, green))
            done = front_layer(slab, state)
            state = []
            for h in range(2):
                run = part[d, 3, x, h]
                state.append((run, jnp.exp2(run * (-rate)), *done[h][2:]))
            store(d, x, back_layer(slab, state))

    def whole(d):
        def column(x, _):
            slab = 2 * d + x + 1
            state = front_layer(slab, [(zeros, 1.0, zeros, zeros, zeros)] * 2)
            store(d, x, back_layer(slab, inner_layers(slab, state)))
            return 0

        lax.fori_loop(0, 2, column, 0)

    def send(d):
        return pltpu.make_async_remote_copy(
            coded.at[d], recv.at[me], ps_sem.at[d], pr_sem.at[me],
            device_id={"depth": d}, device_id_type=MESH,
        )

    codes = []
    orders = plan(depths)
    for s in range(depths):
        codes.append(sum(orders[k][s] * depths**k for k in range(depths)))
    power = choose(me, [depths**k for k in range(depths)])

    def target(s):
        return lax.rem(choose(s, codes) // power, depths)

    def early(s, _):
        inner(target(s))
        return 0

    def early_end(s, _):
        d = target(s)
        outer(d)
        send(d).start()
        return 0

    def late(s, _):
        @pl.when(s == EARLY)
        def _():
            @pl.when(has_down)
            def _():
                x_up.wait_recv()
                relayout(0)

            @pl.when(has_up)
            def _():
                x_down.wait_recv()
                relayout(cx + 1)


        d = target(s)
        whole(d)

        @pl.when(s < depths - 1)
        def _():
            send(d).start()

        return 0

    lax.fori_loop(0, FIRST, early, 0)
    z_down.wait_recv()
    z_up.wait_recv()
    lax.fori_loop(0, FIRST, early_end, 0)
    lax.fori_loop(FIRST, depths, late, 0)
    recv[me] = coded[me]

    for s in range(1, depths):
        source = lax.rem(me + s, depths)
        pltpu.make_async_remote_copy(
            coded.at[source], recv.at[source], ps_sem.at[source], pr_sem.at[source],
            device_id={"depth": source}, device_id_type=MESH,
        ).wait_recv()

    for x in range(2):
        run = jnp.zeros((16, 128), jnp.float32)
        colours = [run, run, run]
        for k in range(depths):
            light = jnp.exp2(run * (-rate))
            for channel in range(3):
                colours[channel] += light * decode(recv[k, channel, x], SCALES[channel])
            run = run + decode(recv[k, 3, x], SCALES[3])
        image = [0.5 * SHADE * colour for colour in colours] + [1.0 - jnp.exp2(run * (-rate))]
        for channel in range(4):
            for h in range(2):
                for c in range(8):
                    y = 256 * c + 128 * h
                    o_ref[channel, x : x + 1, y : y + 128] = image[channel][8 * h + c : 8 * h + c + 1]

    pl.when(has_down)(x_down.wait_send)
    pl.when(has_up)(x_up.wait_send)
    z_down.wait_send()
    z_up.wait_send()
    for s in range(1, depths):
        send(lax.rem(me + s, depths)).wait_send()


def shards(volume):
    tiles, depths = lax.axis_size("tile"), lax.axis_size("depth")
    cx, cz, ny = volume.shape
    dma = pltpu.SemaphoreType.DMA
    return pl.pallas_call(
        functools.partial(render_kernel, tiles, depths),
        out_shape=jax.ShapeDtypeStruct((4, cx // depths, ny), jnp.float32),
        in_specs=[pl.BlockSpec(memory_space=pltpu.HBM)],
        out_specs=pl.BlockSpec(memory_space=pltpu.VMEM),
        scratch_shapes=[
            pltpu.VMEM((cx + 2, cz, ny), jnp.bfloat16),
            pltpu.VMEM((cx + 2, 2, LEAD + PITCH * cz, 128), jnp.float32),
            pltpu.VMEM((2, cx, 16, 128), jnp.bfloat16),
            pltpu.VMEM((2, cx, 16, 128), jnp.bfloat16),
            pltpu.VMEM((depths, 4, 2, 2, 8, 128), jnp.float32),
            pltpu.VMEM((depths, 4, 2, 16, 128), jnp.bfloat16),
            pltpu.VMEM((depths, 4, 2, 16, 128), jnp.bfloat16),
            dma((4,)), dma((2,)), dma((2,)), dma((2,)), dma((2,)), dma((depths,)), dma((depths,)),
        ],
        compiler_params=pltpu.CompilerParams(
            collective_id=0, has_side_effects=True, vmem_limit_bytes=52 * 1024 * 1024
        ),
        cost_estimate=pl.CostEstimate(flops=50_000_000, bytes_accessed=2_300_000, transcendentals=5_000_000),
    )(volume)


def solution(mesh):
    in_specs = (P("tile", "depth", None),)
    out_specs = P(None, ("tile", "depth"), None)
    return jax.shard_map(shards, mesh=mesh, in_specs=in_specs, out_specs=out_specs, check_vma=False)
```

```python
import functools
import math

import jax
import jax.numpy as jnp
from jax import lax
from jax.experimental import pallas as pl
from jax.experimental.pallas import tpu as pltpu
from jax.sharding import PartitionSpec as P

OPACITY = 3.0
LIGHT_X = 0.48
LIGHT_Y = 0.6
LIGHT_Z = 0.64
LOG2E = math.log2(math.e)
SHADE = 0.7 * LIGHT_Z
PITCH = 16
LEAD = 8
FIRST = 8
FAR = 4
EDGE = 12
POWER = 12
SCALES = (256.0, 512.0, 256.0, 32.0)
MESH = pl.DeviceIdType.MESH


def encode(value, scale):
    value = value * scale
    fourth = (value * value) * (value * value)
    return fourth * fourth * fourth


def decode(code, scale):
    return jnp.exp2(jnp.log2(code.astype(jnp.float32)) * (1.0 / POWER) - math.log2(scale))


def cell_terms(rate, centre, gx, gy, gz, state):
    run, light, total, skew, green = state
    facing = jnp.abs((gz + (LIGHT_X / LIGHT_Z) * gx) + (LIGHT_Y / LIGHT_Z) * gy)
    norm = lax.rsqrt(((gx * gx + 4.0) + gz * gz) + gy * gy)
    shade = facing * norm + 0.3 / SHADE
    squared = centre * centre
    run = run + squared * pltpu.reciprocal(1.0 + squared, approx=True)
    after = jnp.exp2(run * (-rate))
    weight = (light - after) * shade
    total = total + weight
    skew = skew + weight * jnp.tanh(centre)
    green = green + weight * jnp.exp2(squared * (-LOG2E))
    return run, after, total, skew, green


def render_kernel(
    tiles, depths, v_ref, o_ref, vin, ws, zout, zin, part, coded, recv,
    load_sem, xs_sem, xr_sem, zs_sem, zr_sem, ps_sem, pr_sem,
):
    cx, cz, _ = v_ref.shape
    tile = lax.axis_index("tile")
    me = lax.axis_index("depth")
    tile_up, tile_down = lax.rem(tile + 1, tiles), lax.rem(tile + tiles - 1, tiles)
    has_up, has_down = tile < tiles - 1, tile > 0
    deep_up, deep_down = lax.rem(me + 1, depths), lax.rem(me + depths - 1, depths)
    rate = OPACITY / (cz * depths) * LOG2E

    batch = cx // 4

    def load(i):
        return pltpu.make_async_copy(
            v_ref.at[pl.ds(i * batch, batch)], vin.at[pl.ds(1 + i * batch, batch)], load_sem.at[i]
        )

    for i in range(4):
        load(i).start()

    barrier = pltpu.get_barrier_semaphore()
    for other, there in ((tile_up, has_up), (tile_down, has_down)):

        @pl.when(there)
        def _():
            pl.semaphore_signal(barrier, inc=1, device_id={"tile": other}, device_id_type=MESH)

    for step in range(1, depths):
        pl.semaphore_signal(
            barrier, inc=1, device_id={"depth": lax.rem(me + step, depths)}, device_id_type=MESH
        )
    in_row = lax.broadcasted_iota(jnp.int32, (256, 256), 1)
    out_row = lax.broadcasted_iota(jnp.int32, (256, 256), 0)
    order = jnp.where(in_row == (out_row % 8) * 32 + out_row // 8, 1.0, 0.0).astype(jnp.bfloat16)
    lane = lax.broadcasted_iota(jnp.int32, (8, 128), 1)
    zeros = jnp.zeros((8, 128), jnp.float32)

    def clear(x, _):
        for h in range(2):
            for z in range(cz + 1):
                ws[x, h, pl.ds(LEAD + PITCH * z - 8, 8), :] = zeros
        return 0

    lax.fori_loop(0, cx + 2, clear, 0)
    for x, there in ((0, has_down), (cx + 1, has_up)):

        @pl.when(jnp.logical_not(there))
        def _():
            for h in range(2):
                for z in range(cz):
                    ws[x, h, pl.ds(LEAD + PITCH * z, 8), :] = zeros


    x_down = pltpu.make_async_remote_copy(
        v_ref.at[0], vin.at[cx + 1], xs_sem.at[0], xr_sem.at[0],
        device_id={"tile": tile_down}, device_id_type=MESH,
    )
    x_up = pltpu.make_async_remote_copy(
        v_ref.at[cx - 1], vin.at[0], xs_sem.at[1], xr_sem.at[1],
        device_id={"tile": tile_up}, device_id_type=MESH,
    )
    def relayout(x):
        slab = vin[x]
        stacked = jnp.concatenate([slab[:, 256 * c : 256 * c + 256] for c in range(8)], axis=0)
        out = jnp.dot(order, stacked, preferred_element_type=jnp.float32)
        for z in range(cz):
            for h in range(2):
                ws[x, h, pl.ds(LEAD + PITCH * z, 8), :] = out[8 * z : 8 * z + 8, 128 * h : 128 * h + 128]

    def own_slabs(i, _):
        load(i).wait()
        for x in range(batch):
            relayout(1 + batch * i + x)

        @pl.when(i == 2)
        def _():
            pl.semaphore_wait(barrier, depths - 1 + jnp.where(has_up, 1, 0) + jnp.where(has_down, 1, 0))
            pl.when(has_down)(x_down.start)
            pl.when(has_up)(x_up.start)

        return 0

    lax.fori_loop(0, cx // batch, own_slabs, 0)

    def cell(slab, z, h, shift=0):
        return ws[slab, h, pl.ds(LEAD + PITCH * z + shift, 8), :]

    def pack(x, _):
        for side, z in ((0, 0), (1, cz - 1)):
            rows = jnp.concatenate([cell(x + 1, z, 0), cell(x + 1, z, 1)], axis=0)
            zout[side, x] = rows.astype(jnp.bfloat16)
        return 0

    lax.fori_loop(0, cx, pack, 0)
    z_down = pltpu.make_async_remote_copy(
        zout.at[0], zin.at[1], zs_sem.at[0], zr_sem.at[0],
        device_id={"depth": deep_down}, device_id_type=MESH,
    )
    z_up = pltpu.make_async_remote_copy(
        zout.at[1], zin.at[0], zs_sem.at[1], zr_sem.at[1],
        device_id={"depth": deep_up}, device_id_type=MESH,
    )
    z_down.start()
    z_up.start()

    def y_differences(slab, z):
        first, second = cell(slab, z, 0), cell(slab, z, 1)
        above, below = cell(slab, z, 0, 1), cell(slab, z, 1, -1)
        right_0 = pltpu.roll(jnp.where(lane == 0, second, first), 127, 1)
        right_1 = pltpu.roll(jnp.where(lane == 0, above, second), 127, 1)
        left_0 = pltpu.roll(jnp.where(lane == 127, below, first), 1, 1)
        left_1 = pltpu.roll(jnp.where(lane == 127, first, second), 1, 1)
        return right_0 - left_0, right_1 - left_1

    near = jnp.where(me == 0, 0.0, 1.0)
    far = jnp.where(me == depths - 1, 0.0, 1.0)

    def x_difference(slab, z, h):
        return cell(slab + 1, z, h) - cell(slab - 1, z, h)

    def front_layer(slab, state):
        halo = zin[0, slab - 1].astype(jnp.float32) * near
        gy = y_differences(slab, 0)
        out = []
        for h in range(2):
            gz = cell(slab, 1, h) - halo[8 * h : 8 * h + 8]
            out.append(cell_terms(rate, cell(slab, 0, h), x_difference(slab, 0, h), gy[h], gz, state[h]))
        return out

    def back_layer(slab, state):
        halo = zin[1, slab - 1].astype(jnp.float32) * far
        gy = y_differences(slab, cz - 1)
        out = []
        for h in range(2):
            gz = halo[8 * h : 8 * h + 8] - cell(slab, cz - 2, h)
            out.append(
                cell_terms(rate, cell(slab, cz - 1, h), x_difference(slab, cz - 1, h), gy[h], gz, state[h])
            )
        return out

    def inner_layers(slab, state):
        for z in range(1, cz - 1):
            gy = y_differences(slab, z)
            for h in range(2):
                gz = cell(slab, z + 1, h) - cell(slab, z - 1, h)
                state[h] = cell_terms(rate, cell(slab, z, h), x_difference(slab, z, h), gy[h], gz, state[h])
        return state

    width = 2 * depths
    first, last = me == 0, me == depths - 1
    edges = jnp.where(first | last, 1, 2)
    count = width - 2 - edges
    start = jnp.where(last, 0, 2 * me + 1)
    edge = jnp.where(last | ((lax.rem(me, 2) == 0) & jnp.logical_not(first)), 0, width - 1)
    own = jnp.where(first, 1, 2 * me)

    def target(p):
        turn = jnp.where(p < EDGE, p, p - edges) + FAR
        turn = jnp.where(turn >= count, turn - count, turn)
        inside = start + turn
        inside = jnp.where(inside >= width - 2, inside - (width - 2), inside) + 1
        middle = jnp.where(p == EDGE, edge, width - 1 - edge)
        late = jnp.where(p == width - 2, own, 4 * me + 1 - own)
        at_edge = (p >= EDGE) & (p < EDGE + edges)
        return jnp.where(p >= width - 2, late, jnp.where(at_edge, middle, inside))

    def store(column, state):
        pairs = []
        for run, _, total, skew, green in state:
            pairs.append([encode(v, s) for v, s in zip((total + skew, green, total - skew, run), SCALES)])
        for channel in range(4):
            rows = jnp.concatenate([pairs[0][channel], pairs[1][channel]], axis=0)
            coded[column, channel] = rows.astype(jnp.bfloat16)

    def send(column):
        return pltpu.make_async_remote_copy(
            coded.at[column], recv.at[me, lax.rem(column, 2)], ps_sem.at[column], pr_sem.at[me, lax.rem(column, 2)],
            device_id={"depth": lax.div(column, 2)}, device_id_type=MESH,
        )

    def early(p, _):
        slab = target(p) + 1
        state = []
        for h in range(2):
            squared = cell(slab, 0, h) ** 2
            run = squared * pltpu.reciprocal(1.0 + squared, approx=True)
            state.append((run, jnp.exp2(run * (-rate)), zeros, zeros, zeros))
        state = inner_layers(slab, state)
        for h in range(2):
            run, _, total, skew, green = state[h]
            for channel, value in enumerate((total, skew, green, run)):
                part[p, channel, h] = value
        return 0

    def early_end(i, _):
        columns = [target(2 * i), target(2 * i + 1)]
        for u, column in enumerate(columns):
            p = 2 * i + u
            state = []
            for h in range(2):
                total, skew, green = (part[p, channel, h] for channel in range(3))
                state.append((zeros, 1.0, total, skew, green))
            done = front_layer(column + 1, state)
            state = []
            for h in range(2):
                run = part[p, 3, h]
                state.append((run, jnp.exp2(run * (-rate)), *done[h][2:]))
            store(column, back_layer(column + 1, state))
        for column in columns:
            send(column).start()
        return 0

    def late(p, _):
        @pl.when(p == EDGE)
        def _():
            @pl.when(has_down)
            def _():
                x_up.wait_recv()
                relayout(0)

            @pl.when(has_up)
            def _():
                x_down.wait_recv()
                relayout(cx + 1)

        column = target(p)
        state = front_layer(column + 1, [(zeros, 1.0, zeros, zeros, zeros)] * 2)
        store(column, back_layer(column + 1, inner_layers(column + 1, state)))

        @pl.when(p < width - 2)
        def _():
            send(column).start()

        return 0

    lax.fori_loop(0, FIRST, early, 0)
    z_down.wait_recv()
    z_up.wait_recv()
    lax.fori_loop(0, FIRST // 2, early_end, 0)
    lax.fori_loop(FIRST, width, late, 0)
    for x in range(2):
        recv[me, x] = coded[2 * me + x]

    for s in range(1, depths):
        source = lax.rem(me + s, depths)
        for x in range(2):
            pltpu.make_async_remote_copy(
                coded.at[x], recv.at[source, x], ps_sem.at[x], pr_sem.at[source, x],
                device_id={"depth": source}, device_id_type=MESH,
            ).wait_recv()

    for x in range(2):
        run = jnp.zeros((16, 128), jnp.float32)
        colours = [run, run, run]
        for k in range(depths):
            light = jnp.exp2(run * (-rate))
            for channel in range(3):
                colours[channel] += light * decode(recv[k, x, channel], SCALES[channel])
            run = run + decode(recv[k, x, 3], SCALES[3])
        image = [0.5 * SHADE * colour for colour in colours] + [1.0 - jnp.exp2(run * (-rate))]
        for channel in range(4):
            for h in range(2):
                for c in range(8):
                    y = 256 * c + 128 * h
                    o_ref[channel, x : x + 1, y : y + 128] = image[channel][8 * h + c : 8 * h + c + 1]

    pl.when(has_down)(x_down.wait_send)
    pl.when(has_up)(x_up.wait_send)
    z_down.wait_send()
    z_up.wait_send()
    for s in range(1, depths):
        for x in range(2):
            send(2 * lax.rem(me + s, depths) + x).wait_send()


def shards(volume):
    tiles, depths = lax.axis_size("tile"), lax.axis_size("depth")
    cx, cz, ny = volume.shape
    dma = pltpu.SemaphoreType.DMA
    return pl.pallas_call(
        functools.partial(render_kernel, tiles, depths),
        out_shape=jax.ShapeDtypeStruct((4, cx // depths, ny), jnp.float32),
        in_specs=[pl.BlockSpec(memory_space=pltpu.HBM)],
        out_specs=pl.BlockSpec(memory_space=pltpu.VMEM),
        scratch_shapes=[
            pltpu.VMEM((cx + 2, cz, ny), jnp.bfloat16),
            pltpu.VMEM((cx + 2, 2, LEAD + PITCH * cz, 128), jnp.float32),
            pltpu.VMEM((2, cx, 16, 128), jnp.bfloat16),
            pltpu.VMEM((2, cx, 16, 128), jnp.bfloat16),
            pltpu.VMEM((FIRST, 4, 2, 8, 128), jnp.float32),
            pltpu.VMEM((cx, 4, 16, 128), jnp.bfloat16),
            pltpu.VMEM((depths, 2, 4, 16, 128), jnp.bfloat16),
            dma((4,)), dma((2,)), dma((2,)), dma((2,)), dma((2,)), dma((cx,)), dma((depths, 2)),
        ],
        compiler_params=pltpu.CompilerParams(
            collective_id=0, has_side_effects=True, vmem_limit_bytes=52 * 1024 * 1024
        ),
        cost_estimate=pl.CostEstimate(flops=50_000_000, bytes_accessed=2_300_000, transcendentals=5_000_000),
    )(volume)


def solution(mesh):
    in_specs = (P("tile", "depth", None),)
    out_specs = P(None, ("tile", "depth"), None)
    return jax.shard_map(shards, mesh=mesh, in_specs=in_specs, out_specs=out_specs, check_vma=False)
```
